256 devices in a mesh: dp: 64 (over y_lo, x, z), mp: 4 (over y_hi, core).
Axes of the slice: x: 4, y: 4 (y_hi: 2, y_lo: 2; y = y_hi * 2 + y_lo), z: 8, core: 2. Of those that a mesh axis runs over, the one named last changes fastest.
Arguments:
- queries: bfloat16 [8192, 4096], P('dp', 'mp'), may hold values from -1 to 1
- passages: bfloat16 [8192, 4096], P('dp', 'mp'), may hold values from -1 to 1
- row_lse: float32 [8192], P('dp'), may hold values from 10 to 11
- row_weight: float32 [8192], P('dp'), may hold values from 0.5 to 2
- positive: int32 [8192], P('dp'), may hold values from 0 to 8191, as said below
Outputs:
- query_grad: bfloat16 [8192, 4096], P('dp', 'mp')
- passage_grad: bfloat16 [8192, 4096], P('dp', 'mp')
The draws below stay inside these ranges and needn't reach their ends.
Inputs may be any that keep to these rules, and one draw needn't show every extreme that they name: Each passage is the positive of exactly one query.
All inputs are finite; a program needn't handle non-finite values.
Results may differ from the reference program's by a relative error of at most 0.005.
Values may be sent and summed in bfloat16 or wider, within the bound.
No kernel may reach another device: no remote copies, remote signals or barrier semaphores. Data moves between devices by JAX's collectives and lax.ppermute only.
A program may use at most 128 MiB of HBM per device.

```python
import math
import jax
import jax.numpy as jnp
from jax import lax

D = 4096
ROWS = 128
BATCH = 8192
N_DP = 64


def shared_rows(key):
    passage_key = jax.random.fold_in(key, 11)
    order_key = jax.random.fold_in(key, 12)
    common_key = jax.random.fold_in(key, 13)
    embedded = jax.random.normal(passage_key, (BATCH, D), jnp.float32) * D ** (-0.5)
    common = jax.random.normal(common_key, (2, D), jnp.float32) * D ** (-0.5)
    order = jax.random.permutation(order_key, BATCH).astype(jnp.int32)
    return (embedded, common, order)


def draw_passages(key, part):
    embedded, common, order = shared_rows(key)
    mixed = 0.5 * common[0][None, :] + embedded
    return jnp.clip(mixed, -1.0, 1.0).astype(jnp.bfloat16)


def draw_positive(key, part):
    embedded, common, order = shared_rows(key)
    return order


def draw_queries(key, part):
    embedded, common, order = shared_rows(key)
    key = jax.random.fold_in(key, 3)
    hard_key, hard_coef_key, pos_key, spread_key, mass_key, noise_key = jax.random.split(key, 6)
    hardest = jax.random.randint(hard_key, (2, BATCH), 0, BATCH)
    coef_hard = jax.random.uniform(hard_coef_key, (2, BATCH, 1), jnp.float32, 0.04, 0.12)
    pos_score = jax.random.uniform(pos_key, (BATCH, 1), jnp.float32, 9.0, 11.0)
    spread = jax.random.uniform(spread_key, (BATCH, 1), jnp.float32, 1.0, 1.8)
    mass = jax.random.uniform(mass_key, (BATCH, 1), jnp.float32, 0.4, 1.0)
    norm_q = spread * (math.sqrt(D) / 50.0)
    shift = 10.5 + jnp.log(mass) - math.log(BATCH) - 0.5 * spread * spread
    coef_common = shift / 25.0
    coef_pos = (pos_score - shift) / 50.0
    coef_shared = 0.3 * norm_q
    rest = norm_q * norm_q - coef_pos * coef_pos - coef_shared * coef_shared - coef_hard[0] * coef_hard[0] - coef_hard[1] * coef_hard[1]
    coef_noise = jnp.sqrt(jnp.maximum(rest, 0.01 * norm_q * norm_q))
    noise = jax.random.normal(noise_key, (BATCH, D), jnp.float32) * D ** (-0.5)
    mixed = coef_pos * embedded[order] + coef_hard[0] * embedded[hardest[0]] + coef_hard[1] * embedded[hardest[1]]
    mixed = mixed + coef_common * common[0][None, :] + coef_shared * common[1][None, :] + coef_noise * noise
    return jnp.clip(mixed, -1.0, 1.0).astype(jnp.bfloat16)


def steps_of(own_key, shape, cuts, low, high):
    def one(axis_at, shards_of):
        draws = jax.random.uniform(jax.random.fold_in(jax.random.fold_in(own_key, 6), axis_at), (shards_of,), jnp.float32, low / len(cuts), high / len(cuts))
        return jnp.repeat(jnp.exp(draws), shape[axis_at] // shards_of).reshape((-1,) + (1,) * (len(shape) - axis_at - 1))

    loudness = one(*cuts[0])
    for cut in cuts[1:]:
        loudness = loudness * one(*cut)
    return loudness


def setup_inputs(seed: int = 0) -> dict:
    key_of = jax.random.split(jax.random.key(seed), 6)
    queries = draw_queries(jax.random.fold_in(key_of[5], 71), 0)
    passages = draw_passages(jax.random.fold_in(key_of[5], 71), 0)
    row_lse = jnp.clip(10.0 + 1.0 * jax.random.uniform(key_of[2], (BATCH,), jnp.float32) ** steps_of(key_of[2], (BATCH,), ((0, 64),), -0.2, 0.2), 10.0, 11.0)
    row_weight = jnp.clip(jnp.exp(math.log(2.0) - 1.3862944 * jax.random.uniform(key_of[3], (BATCH,), jnp.float32) ** steps_of(key_of[3], (BATCH,), ((0, 64),), -0.2, 0.2)), 0.5, 2.0)
    positive = draw_positive(jax.random.fold_in(key_of[5], 71), 0)
    return dict(queries=queries, passages=passages, row_lse=row_lse, row_weight=row_weight, positive=positive)


inv_temp = 50.0


def reference(queries, passages, row_lse, row_weight, positive):
    columns = jnp.arange(BATCH, dtype=jnp.int32)

    def block(carry, block_index):
        first_row = (block_index * ROWS).astype(jnp.int32)
        query_block = lax.dynamic_slice_in_dim(queries, first_row, ROWS, 0)
        lse_block = lax.dynamic_slice_in_dim(row_lse, first_row, ROWS, 0)
        weight_block = lax.dynamic_slice_in_dim(row_weight, first_row, ROWS, 0)
        target_block = lax.dynamic_slice_in_dim(positive, first_row, ROWS, 0)
        scores = inv_temp * lax.dot_general(query_block, passages, (((1,), (1,)), ((), ())), preferred_element_type=jnp.float32)
        is_positive = (columns[None, :] == target_block[:, None]).astype(jnp.float32)
        grads = (weight_block[:, None] * (jnp.exp(scores - lse_block[:, None]) - is_positive)).astype(jnp.bfloat16)
        query_rows = (inv_temp * jnp.dot(grads, passages, preferred_element_type=jnp.float32)).astype(jnp.bfloat16)
        carry = carry + lax.dot_general(grads, query_block, (((0,), (0,)), ((), ())), preferred_element_type=jnp.float32)
        return carry, query_rows

    start_carry = jnp.zeros((BATCH, D), jnp.float32)
    total, query_blocks = lax.scan(block, start_carry, jnp.arange(N_DP, dtype=jnp.int32))
    query_grad = query_blocks.reshape(BATCH, D)
    passage_grad = (inv_temp * total).astype(jnp.bfloat16)
    return query_grad, passage_grad
```

```python
import jax
import jax.numpy as jnp
from jax import lax
from jax.sharding import Mesh, PartitionSpec as P

inv_temp = 50.0
X = "x"
Y = ("yl", "yh")
Z = "z"
ROWS_SPEC = ("yl", "x", "z")
FEATURES_SPEC = ("yh", "c")
bf16, f32 = jnp.bfloat16, jnp.float32


def flip(value, axis, bits):
    if axis is Y:
        bits = bits % 2 * 2 + bits // 2
    return lax.ppermute(value, axis, [(i, i ^ bits) for i in range(4)])


def shift(value, step):
    return lax.ppermute(value, Z, [(i, (i + step) % 8) for i in range(8)])


def gather_four(value, axis):
    half = value.shape[0] // 2
    one, three = flip(value, axis, 1), flip(value, axis, 3)
    first = flip(three[:half], axis, 1)
    second = flip(one[half:], axis, 3)
    return [value, one, jnp.concatenate([first, second]), three]


def scatter_four(parts, axis):
    own, one, two, three = parts
    half = two.shape[0] // 2
    first = flip(two[:half].astype(bf16), axis, 1)
    second = flip(two[half:].astype(bf16), axis, 3)
    three = jnp.concatenate([three[:half] + first, three[half:]]).astype(bf16)
    one = jnp.concatenate([one[:half], one[half:] + second]).astype(bf16)
    return own + flip(three, axis, 3).astype(f32) + flip(one, axis, 1)


def gather_ring(value, plus_steps):
    blocks = [value] + [None] * 7
    up = down = value
    for step in range(1, 5):
        if step <= plus_steps:
            up = shift(up, 1)
            blocks[8 - step] = up
        if step <= 7 - plus_steps:
            down = shift(down, -1)
            blocks[step] = down
    return jnp.concatenate(blocks)


def scatter_ring(parts, plus_steps):
    up = down = None
    for step in range(4, 0, -1):
        if step <= plus_steps:
            mine = parts[step] if up is None else parts[step] + up
            up = shift(mine.astype(bf16), 1)
        if step <= 7 - plus_steps:
            mine = parts[8 - step] if down is None else parts[8 - step] + down
            down = shift(mine.astype(bf16), -1)
    return parts[0] + up.astype(f32) + down


def dot(a, b, contract):
    return lax.dot_general(a, b, (contract, ((), ())), preferred_element_type=f32)


def by_difference(values, x, yl):
    values = jnp.where(yl == 1, values[::-1], values)
    values = jnp.where(x % 2 == 1, values[:, jnp.array([1, 0, 3, 2])], values)
    return jnp.where(x // 2 == 1, values[:, jnp.array([2, 3, 0, 1])], values)


def on_device(queries, passages, row_lse, row_weight, positive):
    x, z, yl, yh = (lax.axis_index(a) for a in (X, Z, "yl", "yh"))
    half = queries.shape[0] // 2

    passage_same = lax.dynamic_slice_in_dim(passages, yh * half, half, 0)
    passage_away = lax.dynamic_slice_in_dim(passages, (1 - yh) * half, half, 0)
    passage_other = flip(passage_away, Y, 2)

    stats = jnp.stack([row_lse, row_weight, positive.astype(f32)])
    stats = lax.all_gather(stats, ("yl", "x"), axis=0, tiled=False)
    stats = by_difference(stats.reshape(2, 4, 3, 2 * half), x, yl)
    stats = jnp.concatenate(
        [
            stats[..., :half].transpose(2, 0, 1, 3).reshape(3, -1),
            stats[..., half:].transpose(2, 1, 0, 3).reshape(3, -1),
        ],
        axis=1,
    )

    first = jnp.concatenate(gather_four(queries[:half], X))
    second = jnp.concatenate(gather_four(queries[half:], Y))
    first = gather_four(first, Y)
    second = gather_four(second, X)
    p_same = gather_ring(passage_same, 4)
    p_other = gather_ring(passage_other, 3)

    q_same = jnp.concatenate([first[0], first[1]] + [b[: 2 * half] for b in second])
    q_other = jnp.concatenate([first[2], first[3]] + [b[2 * half :] for b in second])

    partial_value = dot(q_same, p_same, ((1,), (1,))) + dot(q_other, p_other, ((1,), (1,)))
    scores = partial_value + lax.ppermute(partial_value, "c", [(0, 1), (1, 0)])

    place = jnp.arange(8 * half, dtype=jnp.int32)
    owner = (yl * 4 + x) * 8 + (z + place // half) % 8
    column = (owner * (2 * half) + yh * half + place % half).astype(f32)
    grads = (
        stats[1][:, None]
        * (jnp.exp(inv_temp * scores - stats[0][:, None]) - (column[None, :] == stats[2][:, None]).astype(f32))
    ).astype(bf16)

    v_other = dot(grads, q_other, ((0,), (0,))).reshape(8, half, -1)
    v_same = dot(grads, q_same, ((0,), (0,))).reshape(8, half, -1)
    w_same = dot(grads, p_same, ((1,), (0,)))
    w_other = dot(grads, p_other, ((1,), (0,)))

    passage_away = (inv_temp * scatter_ring(v_other, 3)).astype(bf16)
    passage_own = (inv_temp * scatter_ring(v_same, 4)).astype(bf16)
    passage_back = flip(passage_away, Y, 2)
    passage_grad = jnp.where(
        yh == 0,
        jnp.concatenate([passage_own, passage_back]),
        jnp.concatenate([passage_back, passage_own]),
    )

    block = 4 * half
    first = scatter_four([w_same[:block], w_same[block : 2 * block], w_other[:block], w_other[block : 2 * block]], Y)
    second_same = w_same[2 * block :].reshape(4, 2 * half, -1)
    second_other = w_other[2 * block :].reshape(4, 2 * half, -1)
    second = scatter_four([jnp.concatenate([second_same[e], second_other[e]]) for e in range(4)], X)
    first = scatter_four(list(first.reshape(4, half, -1)), X)
    second = scatter_four(list(second.reshape(4, half, -1)), Y)
    query_grad = (inv_temp * jnp.concatenate([first, second])).astype(bf16)
    return query_grad, passage_grad


def solution(mesh):
    split = Mesh(mesh.devices.reshape(2, 4, 8, 2, 2), ("yl", "x", "z", "yh", "c"))
    matrix, vector = P(ROWS_SPEC, FEATURES_SPEC), P(ROWS_SPEC)
    return jax.shard_map(
        on_device,
        mesh=split,
        in_specs=(matrix, matrix, vector, vector, vector),
        out_specs=(matrix, matrix),
        check_vma=False,
    )
```

```python
import jax
import jax.numpy as jnp
from jax import lax
from jax.sharding import Mesh, PartitionSpec as P

inv_temp = 50.0
ROWS_SPEC = ("yl", "x", "z")
FEATURES_SPEC = ("yh", "c")
PLANE = ("yl", "x", "yh", "c")
bf16, f32 = jnp.bfloat16, jnp.float32
NEAR, FAR = (1, 3), (3, 1)


def flip(value, axis, bits):
    pairs = []
    for yl in range(2):
        for x in range(4):
            for yh in range(2):
                for core in range(2):
                    x_to, y_to = x, 2 * yh + yl
                    if axis == "x":
                        x_to ^= bits[core]
                    else:
                        y_to ^= bits[core]
                    target = (((y_to % 2) * 4 + x_to) * 2 + y_to // 2) * 2 + core
                    pairs.append((((yl * 4 + x) * 2 + yh) * 2 + core, target))
    return lax.ppermute(value, PLANE, pairs)


def shift(value, step):
    return lax.ppermute(value, "z", [(i, (i + step) % 8) for i in range(8)])


def gather_four(value, axis, core):
    rows = value.shape[0]
    near = flip(value, axis, NEAR)
    far = flip(jnp.concatenate([value, near]), axis, FAR)
    one = jnp.where(core == 0, near, far[:rows])
    three = jnp.where(core == 0, far[:rows], near)
    return [value, one, far[rows:], three]


def scatter_four(parts, axis, core):
    own, one, two, three = parts
    rows = own.shape[0]
    near = jnp.where(core == 0, one, three)
    far = jnp.where(core == 0, three, one)
    got = flip(jnp.concatenate([far, two]).astype(bf16), axis, FAR)
    last = flip((near + got[rows:]).astype(bf16), axis, NEAR)
    return own + got[:rows] + last


def gather_ring(value):
    half = value.shape[0] // 2
    blocks = [value] + [None] * 7
    up = down = value
    for step in range(1, 4):
        up, down = shift(up, 1), shift(down, -1)
        blocks[8 - step], blocks[step] = up, down
    blocks[4] = jnp.concatenate([shift(up[:half], 1), shift(down[half:], -1)])
    return blocks


def scatter_ring(parts):
    half = parts[0].shape[0] // 2
    up = shift(parts[4][:half].astype(bf16), 1)
    down = shift(parts[4][half:].astype(bf16), -1)
    up = jnp.concatenate([parts[3][:half] + up, parts[3][half:]]).astype(bf16)
    down = jnp.concatenate([parts[5][:half], parts[5][half:] + down]).astype(bf16)
    up, down = shift(up, 1), shift(down, -1)
    for step in (2, 1):
        up = shift((parts[step] + up).astype(bf16), 1)
        down = shift((parts[8 - step] + down).astype(bf16), -1)
    return parts[0] + up + down


def dot(a, b, contract):
    return lax.dot_general(a, b, (contract, ((), ())), preferred_element_type=f32)


def thirds(value):
    high = lax.reduce_precision(value, 8, 7)
    middle = lax.reduce_precision(value - high, 8, 7)
    return [high, middle, value - high - middle]


def on_device(queries, passages, row_lse, row_weight, positive):
    x, z, yl, yh, core = (lax.axis_index(a) for a in ("x", "z", "yl", "yh", "c"))
    rows, width = queries.shape
    half = rows // 2

    passage_own = lax.dynamic_slice_in_dim(passages, yh * half, half, 0)
    passage_away = lax.dynamic_slice_in_dim(passages, (1 - yh) * half, half, 0)
    passage_back = flip(passage_away, "y", (2, 2))

    target = [(positive // 128).astype(f32), (positive % 128).astype(f32)]
    stats = jnp.stack(thirds(row_lse) + thirds(row_weight) + target, axis=1).astype(bf16)
    loaded = jnp.concatenate([queries, jnp.pad(stats, ((0, 0), (0, 120)))], axis=1)

    first = gather_four(jnp.concatenate(gather_four(loaded[:half], "x", core)), "y", core)
    second = gather_four(jnp.concatenate(gather_four(loaded[half:], "y", core)), "x", core)
    ring = gather_ring(jnp.concatenate([passage_own, passage_back]))
    p_same = jnp.concatenate([b[:half] for b in ring])
    p_other = jnp.concatenate([b[half:] for b in ring])

    q_same = [jnp.concatenate(first[:2]), jnp.concatenate([b[:rows] for b in second])]
    q_other = [jnp.concatenate(first[2:]), jnp.concatenate([b[rows:] for b in second])]
    stats = [q[:, width:].astype(f32) for q in q_same]
    q_same = [q[:, :width] for q in q_same]
    q_other = [q[:, :width] for q in q_other]

    place = jnp.arange(8 * half, dtype=jnp.int32)
    owner = (yl * 4 + x) * 8 + (z + place // half) % 8
    column = owner * rows + yh * half + place % half
    grads = []
    for same, other, stat in zip(q_same, q_other, stats):
        partial_value = dot(same, p_same, ((1,), (1,))) + dot(other, p_other, ((1,), (1,)))
        scores = partial_value + lax.ppermute(partial_value, "c", [(0, 1), (1, 0)])
        lse = stat[:, 0:1] + stat[:, 1:2] + stat[:, 2:3]
        weight = stat[:, 3:4] + stat[:, 4:5] + stat[:, 5:6]
        target = (stat[:, 6:7] * 128 + stat[:, 7:8]).astype(jnp.int32)
        is_positive = (column[None, :] == target).astype(f32)
        grads.append((weight * (jnp.exp(inv_temp * scores - lse) - is_positive)).astype(bf16))

    v_same = dot(grads[0], q_same[0], ((0,), (0,))) + dot(grads[1], q_same[1], ((0,), (0,)))
    v_other = dot(grads[0], q_other[0], ((0,), (0,))) + dot(grads[1], q_other[1], ((0,), (0,)))
    parts = [
        jnp.concatenate([v_same[i * half : (i + 1) * half], v_other[i * half : (i + 1) * half]]) for i in range(8)
    ]
    passage_sum = (inv_temp * scatter_ring(parts)).astype(bf16)
    passage_own = passage_sum[:half]
    passage_back = flip(passage_sum[half:], "y", (2, 2))
    passage_grad = jnp.where(
        yh == 0,
        jnp.concatenate([passage_own, passage_back]),
        jnp.concatenate([passage_back, passage_own]),
    )

    block = 4 * half
    w_same = [dot(g, p_same, ((1,), (0,))) for g in grads]
    w_other = [dot(g, p_other, ((1,), (0,))) for g in grads]
    first = [w_same[0][:block], w_same[0][block:], w_other[0][:block], w_other[0][block:]]
    second = [
        jnp.concatenate([w_same[1][i * rows : (i + 1) * rows], w_other[1][i * rows : (i + 1) * rows]])
        for i in range(4)
    ]
    first = scatter_four(first, "y", core)
    second = scatter_four(second, "x", core)
    first = scatter_four([first[i * half : (i + 1) * half] for i in range(4)], "x", core)
    second = scatter_four([second[i * half : (i + 1) * half] for i in range(4)], "y", core)
    query_grad = (inv_temp * jnp.concatenate([first, second])).astype(bf16)
    return query_grad, passage_grad


def solution(mesh):
    split = Mesh(mesh.devices.reshape(2, 4, 8, 2, 2), ("yl", "x", "z", "yh", "c"))
    matrix, vector = P(ROWS_SPEC, FEATURES_SPEC), P(ROWS_SPEC)
    return jax.shard_map(
        on_device,
        mesh=split,
        in_specs=(matrix, matrix, vector, vector, vector),
        out_specs=(matrix, matrix),
        check_vma=False,
    )
```

```python
import jax
import jax.numpy as jnp
from jax import lax
from jax.experimental import pallas as pl
from jax.experimental.pallas import tpu as pltpu
from jax.sharding import Mesh, PartitionSpec as P

inv_temp = 50.0
ROWS_SPEC = ("yl", "x", "z")
FEATURES_SPEC = ("yh", "c")
PLANE = ("yl", "x", "yh", "c")
bf16, f32 = jnp.bfloat16, jnp.float32
NEAR, FAR = (1, 3), (3, 1)
HALF, WIDTH, LOADED = 64, 1024, 1152
BLOCK, COLUMNS = 256, 512
VMEM, SMEM = pltpu.VMEM, pltpu.SMEM


def flip(value, axis, bits):
    pairs = []
    for yl in range(2):
        for x in range(4):
            for yh in range(2):
                for core in range(2):
                    x_to, y_to = x, 2 * yh + yl
                    if axis == "x":
                        x_to ^= bits[core]
                    else:
                        y_to ^= bits[core]
                    target = (((y_to % 2) * 4 + x_to) * 2 + y_to // 2) * 2 + core
                    pairs.append((((yl * 4 + x) * 2 + yh) * 2 + core, target))
    return lax.ppermute(value, PLANE, pairs)


def shift(value, step):
    return lax.ppermute(value, "z", [(i, (i + step) % 8) for i in range(8)])


def together(*values):
    return lax.optimization_barrier(values)


def dot(a, b, contract):
    return lax.dot_general(a, b, (contract, ((), ())), preferred_element_type=f32)


def prepare(yh_ref, queries, passages, lse, weight, positive, top, low, own, away, need, ready):
    first = yh_ref[0] == 0
    need(1)
    away[...] = jnp.where(first, passages[HALF:, :], passages[0:HALF, :])
    ready(3)
    own[...] = jnp.where(first, passages[0:HALF, :], passages[HALF:, :])
    ready(2)
    need(2, 3, 4)
    rows = []
    for value in (lse[...], weight[...]):
        high = value.astype(bf16).astype(f32)
        middle = (value - high).astype(bf16).astype(f32)
        rows += [high, middle, value - high - middle]
    target = positive[...]
    rows += [(target // 128).astype(f32), (target % 128).astype(f32), jnp.zeros((120, 128), f32)]
    stats = jnp.concatenate(rows).T.astype(bf16)
    need(0)
    top[:, :WIDTH], top[:, WIDTH:] = queries[0:HALF, :], stats[0:HALF]
    low[:, :WIDTH], low[:, WIDTH:] = queries[HALF:, :], stats[HALF:]
    ready(0, 1)


def call(kernel, outs, args, flops=0):
    outs = [jax.ShapeDtypeStruct(*o) for o in outs]
    size = sum(a.size * a.dtype.itemsize for a in [*args, *outs])
    n, m = len(args) - 1, len(outs)

    def body(scalar, *refs):
        operands, results, refs = refs[:n], refs[n : n + m], refs[n + m :]
        here, made, sem_in, sem_out = refs[:n], refs[n : n + m], refs[-2], refs[-1]
        fetched = [pltpu.make_async_copy(operands[i], here[i], sem_in.at[i]) for i in range(n)]
        for copy in fetched:
            copy.start()
        sent = [pltpu.make_async_copy(made[i], results[i], sem_out.at[i]) for i in range(m)]

        def need(*places):
            for i in places:
                fetched[i].wait()

        def ready(*places):
            for i in places:
                sent[i].start()

        kernel(scalar, *here, *made, need=need, ready=ready)
        for copy in sent:
            copy.wait()

    return pl.pallas_call(
        body,
        out_shape=outs,
        in_specs=[pl.BlockSpec(memory_space=s) for s in [SMEM] + [pl.ANY] * n],
        out_specs=[pl.BlockSpec(memory_space=pl.ANY)] * m,
        scratch_shapes=[
            *[VMEM(a.shape, a.dtype) for a in [*args[1:], *outs]],
            pltpu.SemaphoreType.DMA((n,)),
            pltpu.SemaphoreType.DMA((m,)),
        ],
        compiler_params=pltpu.CompilerParams(vmem_limit_bytes=60 * 1024 * 1024),
        cost_estimate=pl.CostEstimate(flops=flops, bytes_accessed=size, transcendentals=0),
    )(*args)


def on_device(queries, passages, row_lse, row_weight, positive):
    x, z, yl, yh, core = (lax.axis_index(a) for a in ("x", "z", "yl", "yh", "c"))
    rows, half = 2 * HALF, HALF
    first_core = core == 0

    vectors = [value.reshape(1, rows) for value in (row_lse, row_weight, positive)]
    quarter = ((half, WIDTH), bf16)
    top, low, passage_own, passage_away = call(
        prepare,
        [((half, LOADED), bf16)] * 2 + [quarter] * 2,
        [yh.astype(jnp.int32).reshape(1), queries, passages, *vectors],
    )
    place = jnp.arange(COLUMNS, dtype=jnp.int32)
    owner = (yl * 4 + x) * 8 + (z + place // half) % 8
    column = (owner * rows + yh * half + place % half)[None, :]

    passage_back, top_near, low_near = together(
        flip(passage_away, "y", (2, 2)), flip(top, "x", NEAR), flip(low, "y", NEAR)
    )
    ring = [None] * 8
    ring[0], top, low = together(
        jnp.concatenate([passage_own, passage_back]),
        jnp.concatenate([top, top_near]),
        jnp.concatenate([low, low_near]),
    )
    ring[7], ring[1], top_far, low_far = together(
        shift(ring[0], 1), shift(ring[0], -1), flip(top, "x", FAR), flip(low, "y", FAR)
    )
    top, low = together(jnp.concatenate([top, top_far]), jnp.concatenate([low, low_far]))
    ring[6], ring[2], top_near, low_near = together(
        shift(ring[7], 1), shift(ring[1], -1), flip(top, "y", NEAR), flip(low, "x", NEAR)
    )
    top, low = together(jnp.concatenate([top, top_near]), jnp.concatenate([low, low_near]))
    top_far, low_far = flip(top, "y", FAR), flip(low, "x", FAR)
    ring[5], ring[3] = together(shift(ring[6], 1), shift(ring[2], -1))
    ring[4] = shift(ring[5], 1)

    p_same = jnp.concatenate([b[:half] for b in ring])
    p_other = jnp.concatenate([b[half:] for b in ring])

    def pick(own, near, far, opposite, axis):
        same = jnp.concatenate([own, jnp.where(first_core, near, far)], axis=axis)
        other = jnp.concatenate([opposite, jnp.where(first_core, far, near)], axis=axis)
        return same, other

    top_same, top_other = pick(top[:BLOCK], top[BLOCK:], top_far[:BLOCK], top_far[BLOCK:], 0)
    low_same, low_other = [], []
    for part in (low, low_far):
        part = part.reshape(2, 4, half, LOADED)
        same, other = pick(part[:, 0:1], part[:, 1:2], part[:, 2:3], part[:, 3:4], 1)
        low_same.append(same.reshape(BLOCK, LOADED))
        low_other.append(other.reshape(BLOCK, LOADED))
    q_same = [top_same, jnp.concatenate(low_same)]
    q_other = [top_other, jnp.concatenate(low_other)]
    stats = [q[:, WIDTH:].astype(f32) for q in q_same]
    q_same = [q[:, :WIDTH] for q in q_same]
    q_other = [q[:, :WIDTH] for q in q_other]

    def swapped(scores, shape, axis):
        scores = lax.ppermute(scores, "c", [(0, 1), (1, 0)]).reshape(shape)
        blocks = [lax.slice_in_dim(scores, i, i + 1, axis=axis) for i in (0, 2, 1, 3)]
        return jnp.concatenate(blocks, axis=axis).reshape(COLUMNS, COLUMNS)

    grads = []
    for same, other, stat, shape, axis in zip(
        q_same, q_other, stats, ((2, 4, half, COLUMNS), (4, rows, COLUMNS)), (1, 0)
    ):
        partial_value = dot(same, p_same, ((1,), (1,))) + dot(other, p_other, ((1,), (1,)))
        scores = partial_value + swapped(partial_value, shape, axis)
        lse = stat[:, 0:1] + stat[:, 1:2] + stat[:, 2:3]
        weight = stat[:, 3:4] + stat[:, 4:5] + stat[:, 5:6]
        target = (stat[:, 6:7] * 128 + stat[:, 7:8]).astype(jnp.int32)
        is_positive = (column == target).astype(f32)
        grads.append((weight * (jnp.exp(inv_temp * scores - lse) - is_positive)).astype(bf16))

    w_same = [dot(g, p_same, ((1,), (0,))) for g in grads]
    w_other = [dot(g, p_other, ((1,), (0,))) for g in grads]
    v_same = dot(grads[0], q_same[0], ((0,), (0,))) + dot(grads[1], q_same[1], ((0,), (0,)))
    v_other = dot(grads[0], q_other[0], ((0,), (0,))) + dot(grads[1], q_other[1], ((0,), (0,)))
    parts = [
        jnp.concatenate([v_same[i * half : (i + 1) * half], v_other[i * half : (i + 1) * half]]) for i in range(8)
    ]

    near, far = w_same[0][BLOCK:], w_other[0][BLOCK:]
    top_own, top_near = w_same[0][:BLOCK], jnp.where(first_core, near, far)
    top_send = jnp.concatenate([jnp.where(first_core, far, near), w_other[0][:BLOCK]]).astype(bf16)
    same, other = w_same[1].reshape(4, rows, WIDTH), w_other[1].reshape(4, rows, WIDTH)
    low_all = jnp.concatenate([same, other], axis=1)
    low_own, low_near, low_send = low_all[0], low_all[1], low_all[2:].reshape(2 * BLOCK, WIDTH).astype(bf16)
    top_got, low_got = flip(top_send, "y", FAR), flip(low_send, "x", FAR)
    up, down = together(shift(parts[4].astype(bf16), 1), shift(parts[5].astype(bf16), -1))
    up, down = together((parts[3] + up).astype(bf16), (parts[6] + down).astype(bf16))
    up, down, top_got, low_got = together(shift(up, 1), shift(down, -1), top_got, low_got)
    up, down, top_send, low_send = together(
        (parts[2] + up).astype(bf16),
        (parts[7] + down).astype(bf16),
        (top_near + top_got[BLOCK:]).astype(bf16),
        (low_near + low_got[BLOCK:]).astype(bf16),
    )
    up, down, top_last, low_last = together(
        shift(up, 1), shift(down, -1), flip(top_send, "y", NEAR), flip(low_send, "x", NEAR)
    )
    top = top_own + top_got[:BLOCK] + top_last
    low = low_own + low_got[:BLOCK] + low_last
    one, three = low[half:rows], low[rows + half :]
    low_near = jnp.where(first_core, one, three)
    low_send = jnp.concatenate([jnp.where(first_core, three, one), low[rows : rows + half]]).astype(bf16)
    up, top_send, low_send = together((parts[1] + up).astype(bf16), top[rows:].astype(bf16), low_send)
    up, top_got, low_got = together(shift(up, 1), flip(top_send, "x", FAR), flip(low_send, "y", FAR))
    passage_sum = (inv_temp * (parts[0] + up + down)).astype(bf16)
    passage_own = passage_sum[:half]
    passage_back = flip(passage_sum[half:], "y", (2, 2))
    top_last = flip((top[half:rows] + top_got[half:]).astype(bf16), "x", NEAR)
    low_last = flip((low_near + low_got[half:]).astype(bf16), "y", NEAR)
    passage_grad = jnp.where(
        yh == 0,
        jnp.concatenate([passage_own, passage_back]),
        jnp.concatenate([passage_back, passage_own]),
    )
    top = top[:half] + top_got[:half] + top_last
    low = low[:half] + low_got[:half] + low_last
    query_grad = (inv_temp * jnp.concatenate([top, low])).astype(bf16)
    return query_grad, passage_grad


def solution(mesh):
    split = Mesh(mesh.devices.reshape(2, 4, 8, 2, 2), ("yl", "x", "z", "yh", "c"))
    matrix, vector = P(ROWS_SPEC, FEATURES_SPEC), P(ROWS_SPEC)
    return jax.shard_map(
        on_device,
        mesh=split,
        in_specs=(matrix, matrix, vector, vector, vector),
        out_specs=(matrix, matrix),
        check_vma=False,
    )
```

```python
import jax
import jax.numpy as jnp
import numpy as np
from jax import lax
from jax.experimental import pallas as pl
from jax.experimental.pallas import tpu as pltpu
from jax.sharding import Mesh, PartitionSpec as P

inv_temp = 50.0
ROWS_SPEC = ("yl", "x", "z")
FEATURES_SPEC = ("yh", "c")
PLANE = ("yl", "x", "yh", "c")
bf16, f32 = jnp.bfloat16, jnp.float32
NEAR, FAR = (1, 3), (3, 1)
AROUND = np.array([0, 1, 7, 6, 2, 3, 5, 4], np.int32)
HALF, WIDTH, LOADED = 64, 1024, 1152
BLOCK, COLUMNS = 256, 512
VMEM, SMEM = pltpu.VMEM, pltpu.SMEM


def flip(value, axis, bits):
    pairs = []
    for yl in range(2):
        for x in range(4):
            for yh in range(2):
                for core in range(2):
                    x_to, y_to = x, 2 * yh + yl
                    if axis == "x":
                        x_to ^= bits[core]
                    else:
                        y_to ^= bits[core]
                    target = (((y_to % 2) * 4 + x_to) * 2 + y_to // 2) * 2 + core
                    pairs.append((((yl * 4 + x) * 2 + yh) * 2 + core, target))
    return lax.ppermute(value, PLANE, pairs)


def exchange(value, turn):
    pairs = []
    for z in range(8):
        for core in range(2):
            step = 1 if (turn + core + z) % 2 == 0 else -1
            pairs.append((z * 2 + core, (z + step) % 8 * 2 + core))
    return lax.ppermute(value, ("z", "c"), pairs)


def shift(value, step):
    return lax.ppermute(value, "z", [(i, (i + step) % 8) for i in range(8)])


def together(*values):
    return lax.optimization_barrier(values)


def dot(a, b, contract):
    return lax.dot_general(a, b, (contract, ((), ())), preferred_element_type=f32)


def prepare(yh_ref, queries, passages, lse, weight, positive, top, low, own, away, need, ready):
    first = yh_ref[0] == 0
    need(1)
    away[...] = jnp.where(first, passages[HALF:, :], passages[0:HALF, :])
    ready(3)
    own[...] = jnp.where(first, passages[0:HALF, :], passages[HALF:, :])
    ready(2)
    need(2, 3, 4)
    rows = []
    for value in (lse[...], weight[...]):
        high = value.astype(bf16).astype(f32)
        middle = (value - high).astype(bf16).astype(f32)
        rows += [high, middle, value - high - middle]
    target = positive[...]
    rows += [(target // 128).astype(f32), (target % 128).astype(f32), jnp.zeros((120, 128), f32)]
    stats = jnp.concatenate(rows).T.astype(bf16)
    need(0)
    top[:, :WIDTH], top[:, WIDTH:] = queries[0:HALF, :], stats[0:HALF]
    low[:, :WIDTH], low[:, WIDTH:] = queries[HALF:, :], stats[HALF:]
    ready(0, 1)


def call(kernel, outs, args, flops=0):
    outs = [jax.ShapeDtypeStruct(*o) for o in outs]
    size = sum(a.size * a.dtype.itemsize for a in [*args, *outs])
    n, m = len(args) - 1, len(outs)

    def body(scalar, *refs):
        operands, results, refs = refs[:n], refs[n : n + m], refs[n + m :]
        here, made, sem_in, sem_out = refs[:n], refs[n : n + m], refs[-2], refs[-1]
        fetched = [pltpu.make_async_copy(operands[i], here[i], sem_in.at[i]) for i in range(n)]
        for copy in fetched:
            copy.start()
        sent = [pltpu.make_async_copy(made[i], results[i], sem_out.at[i]) for i in range(m)]

        def need(*places):
            for i in places:
                fetched[i].wait()

        def ready(*places):
            for i in places:
                sent[i].start()

        kernel(scalar, *here, *made, need=need, ready=ready)
        for copy in sent:
            copy.wait()

    return pl.pallas_call(
        body,
        out_shape=outs,
        in_specs=[pl.BlockSpec(memory_space=s) for s in [SMEM] + [pl.ANY] * n],
        out_specs=[pl.BlockSpec(memory_space=pl.ANY)] * m,
        scratch_shapes=[
            *[VMEM(a.shape, a.dtype) for a in [*args[1:], *outs]],
            pltpu.SemaphoreType.DMA((n,)),
            pltpu.SemaphoreType.DMA((m,)),
        ],
        compiler_params=pltpu.CompilerParams(vmem_limit_bytes=60 * 1024 * 1024),
        cost_estimate=pl.CostEstimate(flops=flops, bytes_accessed=size, transcendentals=0),
    )(*args)


def on_device(queries, passages, row_lse, row_weight, positive):
    x, z, yl, yh, core = (lax.axis_index(a) for a in ("x", "z", "yl", "yh", "c"))
    rows, half = 2 * HALF, HALF
    first_core = core == 0

    vectors = [value.reshape(1, rows) for value in (row_lse, row_weight, positive)]
    quarter = ((half, WIDTH), bf16)
    top, low, passage_own, passage_away = call(
        prepare,
        [((half, LOADED), bf16)] * 2 + [quarter] * 2,
        [yh.astype(jnp.int32).reshape(1), queries, passages, *vectors],
    )
    place = jnp.arange(COLUMNS, dtype=jnp.int32)
    owner = (yl * 4 + x) * 8 + (z + np.repeat(AROUND, half)) % 8
    column = (owner * rows + yh * half + place % half)[None, :]

    passage_back = flip(passage_away, "y", (2, 2))
    top_near, low_near = together(flip(top, "x", NEAR), flip(low, "y", NEAR))
    passage = jnp.concatenate([passage_own, passage_back])
    top, low = together(jnp.concatenate([top, top_near]), jnp.concatenate([low, low_near]))
    passage_near, top_far, low_far = together(exchange(passage, 0), flip(top, "x", FAR), flip(low, "y", FAR))
    ring, top, low = together(
        jnp.concatenate([passage, passage_near]),
        jnp.concatenate([top, top_far]),
        jnp.concatenate([low, low_far]),
    )
    got, top_near, low_near = together(exchange(ring, 1), flip(top, "y", NEAR), flip(low, "x", NEAR))
    top, low = together(jnp.concatenate([top, top_near]), jnp.concatenate([low, low_near]))
    top_far, low_far = flip(top, "y", FAR), flip(low, "x", FAR)
    ring = [passage, passage_near, got[:rows], got[rows:]]
    for turn in (0, 1):
        got = exchange(got, turn)
        ring += [got[:rows], got[rows:]]
    plus = (z + core) % 2 == 0

    def in_order(blocks):
        blocks = list(blocks)
        for i in (1, 3, 5):
            one, two = blocks[i : i + 2]
            blocks[i : i + 2] = jnp.where(plus, one, two), jnp.where(plus, two, one)
        return blocks

    ring = in_order(ring)
    p_same = jnp.concatenate([b[:half] for b in ring])
    p_other = jnp.concatenate([b[half:] for b in ring])

    def pick(own, near, far, opposite, axis):
        same = jnp.concatenate([own, jnp.where(first_core, near, far)], axis=axis)
        other = jnp.concatenate([opposite, jnp.where(first_core, far, near)], axis=axis)
        return same, other

    top_same, top_other = pick(top[:BLOCK], top[BLOCK:], top_far[:BLOCK], top_far[BLOCK:], 0)
    low_same, low_other = [], []
    for part in (low, low_far):
        part = part.reshape(2, 4, half, LOADED)
        same, other = pick(part[:, 0:1], part[:, 1:2], part[:, 2:3], part[:, 3:4], 1)
        low_same.append(same.reshape(BLOCK, LOADED))
        low_other.append(other.reshape(BLOCK, LOADED))
    q_same = [top_same, jnp.concatenate(low_same)]
    q_other = [top_other, jnp.concatenate(low_other)]
    stats = [q[:, WIDTH:].astype(f32) for q in q_same]
    q_same = [q[:, :WIDTH] for q in q_same]
    q_other = [q[:, :WIDTH] for q in q_other]

    def swapped(scores, shape, axis):
        scores = lax.ppermute(scores, "c", [(0, 1), (1, 0)]).reshape(shape)
        blocks = [lax.slice_in_dim(scores, i, i + 1, axis=axis) for i in (0, 2, 1, 3)]
        return jnp.concatenate(blocks, axis=axis).reshape(COLUMNS, COLUMNS)

    grads = []
    for same, other, stat, shape, axis in zip(
        q_same, q_other, stats, ((2, 4, half, COLUMNS), (4, rows, COLUMNS)), (1, 0)
    ):
        partial_value = dot(same, p_same, ((1,), (1,))) + dot(other, p_other, ((1,), (1,)))
        scores = partial_value + swapped(partial_value, shape, axis)
        lse = stat[:, 0:1] + stat[:, 1:2] + stat[:, 2:3]
        weight = stat[:, 3:4] + stat[:, 4:5] + stat[:, 5:6]
        target = (stat[:, 6:7] * 128 + stat[:, 7:8]).astype(jnp.int32)
        is_positive = (column == target).astype(f32)
        grads.append((weight * (jnp.exp(inv_temp * scores - lse) - is_positive)).astype(bf16))

    w_same = [dot(g, p_same, ((1,), (0,))) for g in grads]
    w_other = [dot(g, p_other, ((1,), (0,))) for g in grads]
    v_same = dot(grads[0], q_same[0], ((0,), (0,))) + dot(grads[1], q_same[1], ((0,), (0,)))
    v_other = dot(grads[0], q_other[0], ((0,), (0,))) + dot(grads[1], q_other[1], ((0,), (0,)))
    parts = [
        jnp.concatenate([v_same[i * half : (i + 1) * half], v_other[i * half : (i + 1) * half]]) for i in range(8)
    ]

    near, far = w_same[0][BLOCK:], w_other[0][BLOCK:]
    top_own, top_near = w_same[0][:BLOCK], jnp.where(first_core, near, far)
    top_send = jnp.concatenate([jnp.where(first_core, far, near), w_other[0][:BLOCK]]).astype(bf16)
    same, other = w_same[1].reshape(4, rows, WIDTH), w_other[1].reshape(4, rows, WIDTH)
    low_all = jnp.concatenate([same, other], axis=1)
    low_own, low_near, low_send = low_all[0], low_all[1], low_all[2:].reshape(2 * BLOCK, WIDTH).astype(bf16)
    top_got, low_got = flip(top_send, "y", FAR), flip(low_send, "x", FAR)
    parts = dict(zip(AROUND.tolist(), parts))
    up, down = together(shift(parts[4].astype(bf16), 1), shift(parts[5].astype(bf16), -1))
    up, down = together((parts[3] + up).astype(bf16), (parts[6] + down).astype(bf16))
    up, down, top_got, low_got = together(shift(up, 1), shift(down, -1), top_got, low_got)
    up, down, top_send, low_send = together(
        (parts[2] + up).astype(bf16),
        (parts[7] + down).astype(bf16),
        (top_near + top_got[BLOCK:]).astype(bf16),
        (low_near + low_got[BLOCK:]).astype(bf16),
    )
    up, down, top_last, low_last = together(
        shift(up, 1), shift(down, -1), flip(top_send, "y", NEAR), flip(low_send, "x", NEAR)
    )
    top = top_own + top_got[:BLOCK] + top_last
    low = low_own + low_got[:BLOCK] + low_last
    one, three = low[half:rows], low[rows + half :]
    low_near = jnp.where(first_core, one, three)
    low_send = jnp.concatenate([jnp.where(first_core, three, one), low[rows : rows + half]]).astype(bf16)
    up, top_send, low_send = together((parts[1] + up).astype(bf16), top[rows:].astype(bf16), low_send)
    up, top_got, low_got = together(shift(up, 1), flip(top_send, "x", FAR), flip(low_send, "y", FAR))
    passage_sum = (inv_temp * (parts[0] + up + down)).astype(bf16)
    passage_own = passage_sum[:half]
    passage_back = flip(passage_sum[half:], "y", (2, 2))
    top_last = flip((top[half:rows] + top_got[half:]).astype(bf16), "x", NEAR)
    low_last = flip((low_near + low_got[half:]).astype(bf16), "y", NEAR)
    passage_grad = jnp.where(
        yh == 0,
        jnp.concatenate([passage_own, passage_back]),
        jnp.concatenate([passage_back, passage_own]),
    )
    top = (inv_temp * (top[:half] + top_got[:half] + top_last)).astype(bf16)
    low = (inv_temp * (low[:half] + low_got[:half] + low_last)).astype(bf16)
    query_grad = jnp.concatenate([top, low])
    return query_grad, passage_grad


def solution(mesh):
    split = Mesh(mesh.devices.reshape(2, 4, 8, 2, 2), ("yl", "x", "z", "yh", "c"))
    matrix, vector = P(ROWS_SPEC, FEATURES_SPEC), P(ROWS_SPEC)
    return jax.shard_map(
        on_device,
        mesh=split,
        in_specs=(matrix, matrix, vector, vector, vector),
        out_specs=(matrix, matrix),
        check_vma=False,
    )
```

```python
import jax
import jax.numpy as jnp
import numpy as np
from jax import lax
from jax.experimental import pallas as pl
from jax.experimental.pallas import tpu as pltpu
from jax.sharding import Mesh, PartitionSpec as P

inv_temp = 50.0
ROWS_SPEC = ("yl", "x", "z")
FEATURES_SPEC = ("yh", "c")
PLANE = ("yl", "x", "yh", "c")
bf16, f32 = jnp.bfloat16, jnp.float32
NEAR, FAR = (1, 3), (3, 1)
AROUND = np.array([0, 1, 7, 6, 2, 3, 5, 4], np.int32)
HALF, WIDTH, LOADED = 64, 1024, 1152
BLOCK, COLUMNS = 256, 512
VMEM, SMEM = pltpu.VMEM, pltpu.SMEM


def flip(value, axis, bits):
    pairs = []
    for yl in range(2):
        for x in range(4):
            for yh in range(2):
                for core in range(2):
                    x_to, y_to = x, 2 * yh + yl
                    if axis == "x":
                        x_to ^= bits[core]
                    else:
                        y_to ^= bits[core]
                    target = (((y_to % 2) * 4 + x_to) * 2 + y_to // 2) * 2 + core
                    pairs.append((((yl * 4 + x) * 2 + yh) * 2 + core, target))
    return lax.ppermute(value, PLANE, pairs)


def exchange(value, turn):
    pairs = []
    for z in range(8):
        for core in range(2):
            step = 1 if (turn + core + z) % 2 == 0 else -1
            pairs.append((z * 2 + core, (z + step) % 8 * 2 + core))
    return lax.ppermute(value, ("z", "c"), pairs)


def shift(value, step):
    return lax.ppermute(value, "z", [(i, (i + step) % 8) for i in range(8)])


def together(*values):
    return lax.optimization_barrier(values)


def dot(a, b, contract):
    return lax.dot_general(a, b, (contract, ((), ())), preferred_element_type=f32)


def prepare(yh_ref, queries, passages, lse, weight, positive, top, low, own, away, need, ready):
    first = yh_ref[0] == 0
    need(1)
    away[...] = jnp.where(first, passages[HALF:, :], passages[0:HALF, :])
    ready(3)
    own[...] = jnp.where(first, passages[0:HALF, :], passages[HALF:, :])
    ready(2)
    need(2, 3, 4)
    rows = []
    for value in (lse[...], weight[...]):
        high = value.astype(bf16).astype(f32)
        middle = (value - high).astype(bf16).astype(f32)
        rows += [high, middle, value - high - middle]
    target = positive[...]
    rows += [(target // 128).astype(f32), (target % 128).astype(f32), jnp.zeros((120, 128), f32)]
    stats = jnp.concatenate(rows).T.astype(bf16)
    need(0)
    top[:, :WIDTH], top[:, WIDTH:] = queries[0:HALF, :], stats[0:HALF]
    low[:, :WIDTH], low[:, WIDTH:] = queries[HALF:, :], stats[HALF:]
    ready(0, 1)


def call(kernel, outs, args, flops=0):
    outs = [jax.ShapeDtypeStruct(*o) for o in outs]
    size = sum(a.size * a.dtype.itemsize for a in [*args, *outs])
    n, m = len(args) - 1, len(outs)

    def body(scalar, *refs):
        operands, results, refs = refs[:n], refs[n : n + m], refs[n + m :]
        here, made, sem_in, sem_out = refs[:n], refs[n : n + m], refs[-2], refs[-1]
        fetched = [pltpu.make_async_copy(operands[i], here[i], sem_in.at[i]) for i in range(n)]
        for copy in fetched:
            copy.start()
        sent = [pltpu.make_async_copy(made[i], results[i], sem_out.at[i]) for i in range(m)]

        def need(*places):
            for i in places:
                fetched[i].wait()

        def ready(*places):
            for i in places:
                sent[i].start()

        kernel(scalar, *here, *made, need=need, ready=ready)
        for copy in sent:
            copy.wait()

    return pl.pallas_call(
        body,
        out_shape=outs,
        in_specs=[pl.BlockSpec(memory_space=s) for s in [SMEM] + [pl.ANY] * n],
        out_specs=[pl.BlockSpec(memory_space=pl.ANY)] * m,
        scratch_shapes=[
            *[VMEM(a.shape, a.dtype) for a in [*args[1:], *outs]],
            pltpu.SemaphoreType.DMA((n,)),
            pltpu.SemaphoreType.DMA((m,)),
        ],
        compiler_params=pltpu.CompilerParams(vmem_limit_bytes=60 * 1024 * 1024),
        cost_estimate=pl.CostEstimate(flops=flops, bytes_accessed=size, transcendentals=0),
    )(*args)


def on_device(queries, passages, row_lse, row_weight, positive):
    x, z, yl, yh, core = (lax.axis_index(a) for a in ("x", "z", "yl", "yh", "c"))
    rows, half = 2 * HALF, HALF
    flops = 2 * BLOCK * COLUMNS * WIDTH
    first_core = core == 0

    vectors = [value.reshape(1, rows) for value in (row_lse, row_weight, positive)]
    quarter = ((half, WIDTH), bf16)
    top, low, passage_own, passage_away = call(
        prepare,
        [((half, LOADED), bf16)] * 2 + [quarter] * 2,
        [yh.astype(jnp.int32).reshape(1), queries, passages, *vectors],
    )
    place = jnp.arange(COLUMNS, dtype=jnp.int32)
    owner = (yl * 4 + x) * 8 + (z + np.repeat(AROUND, half)) % 8
    column = (owner * rows + yh * half + place % half)[None, :]

    passage_back = flip(passage_away, "y", (2, 2))
    top_near, low_near = together(flip(top, "x", NEAR), flip(low, "y", NEAR))
    passage = jnp.concatenate([passage_own, passage_back])
    top, low = together(jnp.concatenate([top, top_near]), jnp.concatenate([low, low_near]))
    passage_near, top_far, low_far = together(exchange(passage, 0), flip(top, "x", FAR), flip(low, "y", FAR))
    ring, top, low = together(
        jnp.concatenate([passage, passage_near]),
        jnp.concatenate([top, top_far]),
        jnp.concatenate([low, low_far]),
    )
    got, top_near, low_near = together(exchange(ring, 1), flip(top, "y", NEAR), flip(low, "x", NEAR))
    top, low = together(jnp.concatenate([top, top_near]), jnp.concatenate([low, low_near]))
    top_far, low_far = flip(top, "y", FAR), flip(low, "x", FAR)
    ring = [passage, passage_near, got[:rows], got[rows:]]
    for turn in (0, 1):
        got = exchange(got, turn)
        ring += [got[:rows], got[rows:]]
    plus = (z + core) % 2 == 0

    def in_order(blocks):
        blocks = list(blocks)
        for i in (1, 3, 5):
            one, two = blocks[i : i + 2]
            blocks[i : i + 2] = jnp.where(plus, one, two), jnp.where(plus, two, one)
        return blocks

    ring = in_order(ring)
    p_same = jnp.concatenate([b[:half] for b in ring])
    p_other = jnp.concatenate([b[half:] for b in ring])

    def pick(own, near, far, opposite, axis):
        same = jnp.concatenate([own, jnp.where(first_core, near, far)], axis=axis)
        other = jnp.concatenate([opposite, jnp.where(first_core, far, near)], axis=axis)
        return same, other

    top_same, top_other = pick(top[:BLOCK], top[BLOCK:], top_far[:BLOCK], top_far[BLOCK:], 0)
    low_same, low_other = [], []
    for part in (low, low_far):
        part = part.reshape(2, 4, half, LOADED)
        same, other = pick(part[:, 0:1], part[:, 1:2], part[:, 2:3], part[:, 3:4], 1)
        low_same.append(same.reshape(BLOCK, LOADED))
        low_other.append(other.reshape(BLOCK, LOADED))
    q_same = [top_same, jnp.concatenate(low_same)]
    q_other = [top_other, jnp.concatenate(low_other)]
    stats = [q[:, WIDTH:].astype(f32) for q in q_same]
    q_same = [q[:, :WIDTH] for q in q_same]
    q_other = [q[:, :WIDTH] for q in q_other]

    def swapped(scores, shape, axis):
        scores = lax.ppermute(scores, "c", [(0, 1), (1, 0)]).reshape(shape)
        blocks = [lax.slice_in_dim(scores, i, i + 1, axis=axis) for i in (0, 2, 1, 3)]
        return jnp.concatenate(blocks, axis=axis).reshape(COLUMNS, COLUMNS)

    grads = []
    for same, other, stat, shape, axis in zip(
        q_same, q_other, stats, ((2, 4, half, COLUMNS), (4, rows, COLUMNS)), (1, 0)
    ):
        partial_value = dot(same, p_same, ((1,), (1,))) + dot(other, p_other, ((1,), (1,)))
        scores = partial_value + swapped(partial_value, shape, axis)
        lse = stat[:, 0:1] + stat[:, 1:2] + stat[:, 2:3]
        weight = stat[:, 3:4] + stat[:, 4:5] + stat[:, 5:6]
        target = (stat[:, 6:7] * 128 + stat[:, 7:8]).astype(jnp.int32)
        is_positive = (column == target).astype(f32)
        grads.append((weight * (jnp.exp(inv_temp * scores - lse) - is_positive)).astype(bf16))

    w_same = [dot(g, p_same, ((1,), (0,))) for g in grads]
    w_other = [dot(g, p_other, ((1,), (0,))) for g in grads]
    v_same = dot(grads[0], q_same[0], ((0,), (0,))) + dot(grads[1], q_same[1], ((0,), (0,)))
    v_other = dot(grads[0], q_other[0], ((0,), (0,))) + dot(grads[1], q_other[1], ((0,), (0,)))
    parts = [
        jnp.concatenate([v_same[i * half : (i + 1) * half], v_other[i * half : (i + 1) * half]]) for i in range(8)
    ]

    near, far = w_same[0][BLOCK:], w_other[0][BLOCK:]
    top_own, top_near = w_same[0][:BLOCK], jnp.where(first_core, near, far)
    top_send = jnp.concatenate([jnp.where(first_core, far, near), w_other[0][:BLOCK]]).astype(bf16)
    same, other = w_same[1].reshape(4, rows, WIDTH), w_other[1].reshape(4, rows, WIDTH)
    low_all = jnp.concatenate([same, other], axis=1)
    low_own, low_near, low_send = low_all[0], low_all[1], low_all[2:].reshape(2 * BLOCK, WIDTH).astype(bf16)
    top_got, low_got = flip(top_send, "y", FAR), flip(low_send, "x", FAR)
    parts = dict(zip(AROUND.tolist(), parts))
    up, down = together(shift(parts[4].astype(bf16), 1), shift(parts[5].astype(bf16), -1))
    up, down = together((parts[3] + up).astype(bf16), (parts[6] + down).astype(bf16))
    up, down, top_got, low_got = together(shift(up, 1), shift(down, -1), top_got, low_got)
    up, down = together((parts[2] + up).astype(bf16), (parts[7] + down).astype(bf16))
    up, down = together(shift(up, 1), shift(down, -1))
    top_send, low_send = together(
        (top_near + top_got[BLOCK:]).astype(bf16), (low_near + low_got[BLOCK:]).astype(bf16)
    )
    top_last, low_last = together(flip(top_send, "y", NEAR), flip(low_send, "x", NEAR))
    top = top_own + top_got[:BLOCK] + top_last
    low = low_own + low_got[:BLOCK] + low_last
    one, three = low[half:rows], low[rows + half :]
    low_near = jnp.where(first_core, one, three)
    low_send = jnp.concatenate([jnp.where(first_core, three, one), low[rows : rows + half]]).astype(bf16)
    up = shift((parts[1] + up).astype(bf16), 1)
    top_send, low_send = together(top[rows:].astype(bf16), low_send)
    top_got, low_got = together(flip(top_send, "x", FAR), flip(low_send, "y", FAR))
    passage_sum = (inv_temp * (parts[0] + up + down)).astype(bf16)
    passage_own = passage_sum[:half]
    passage_back = flip(passage_sum[half:], "y", (2, 2))
    top_last = flip((top[half:rows] + top_got[half:]).astype(bf16), "x", NEAR)
    low_last = flip((low_near + low_got[half:]).astype(bf16), "y", NEAR)
    passage_back, top_last, low_last = together(passage_back, top_last, low_last)
    passage_grad = jnp.where(
        yh == 0,
        jnp.concatenate([passage_own, passage_back]),
        jnp.concatenate([passage_back, passage_own]),
    )
    top = (inv_temp * (top[:half] + top_got[:half] + top_last)).astype(bf16)
    low = (inv_temp * (low[:half] + low_got[:half] + low_last)).astype(bf16)
    query_grad = jnp.concatenate([top, low])
    return query_grad, passage_grad


def solution(mesh):
    split = Mesh(mesh.devices.reshape(2, 4, 8, 2, 2), ("yl", "x", "z", "yh", "c"))
    matrix, vector = P(ROWS_SPEC, FEATURES_SPEC), P(ROWS_SPEC)
    return jax.shard_map(
        on_device,
        mesh=split,
        in_specs=(matrix, matrix, vector, vector, vector),
        out_specs=(matrix, matrix),
        check_vma=False,
    )
```

```python
import jax
import jax.numpy as jnp
import numpy as np
from jax import lax
from jax.experimental import pallas as pl
from jax.experimental.pallas import tpu as pltpu
from jax.sharding import Mesh, PartitionSpec as P

inv_temp = 50.0
ROWS_SPEC = ("yl", "x", "z")
FEATURES_SPEC = ("yh", "c")
PLANE = ("yl", "x", "yh", "c")
bf16, f32 = jnp.bfloat16, jnp.float32
NEAR, FAR = (1, 3), (3, 1)
AROUND = np.array([0, 1, 7, 6, 2, 3, 5, 4], np.int32)
HALF, WIDTH, LOADED = 64, 1024, 1152
BLOCK, COLUMNS = 256, 512
VMEM, SMEM = pltpu.VMEM, pltpu.SMEM


def flip(value, axis, bits):
    pairs = []
    for yl in range(2):
        for x in range(4):
            for yh in range(2):
                for core in range(2):
                    x_to, y_to = x, 2 * yh + yl
                    if axis == "x":
                        x_to ^= bits[core]
                    else:
                        y_to ^= bits[core]
                    target = (((y_to % 2) * 4 + x_to) * 2 + y_to // 2) * 2 + core
                    pairs.append((((yl * 4 + x) * 2 + yh) * 2 + core, target))
    return lax.ppermute(value, PLANE, pairs)


def exchange(value, turn):
    pairs = []
    for z in range(8):
        for core in range(2):
            step = 1 if (turn + core + z) % 2 == 0 else -1
            pairs.append((z * 2 + core, (z + step) % 8 * 2 + core))
    return lax.ppermute(value, ("z", "c"), pairs)


def shift(value, step):
    return lax.ppermute(value, "z", [(i, (i + step) % 8) for i in range(8)])


def together(*values):
    return lax.optimization_barrier(values)


def dot(a, b, contract):
    return lax.dot_general(a, b, (contract, ((), ())), preferred_element_type=f32)


def prepare(yh_ref, queries, passages, lse, weight, positive, top, low, own, away, need, ready):
    first = yh_ref[0] == 0
    need(1)
    away[...] = jnp.where(first, passages[HALF:, :], passages[0:HALF, :])
    ready(3)
    own[...] = jnp.where(first, passages[0:HALF, :], passages[HALF:, :])
    ready(2)
    need(2, 3, 4)
    rows = []
    for value in (lse[...], weight[...]):
        high = value.astype(bf16).astype(f32)
        middle = (value - high).astype(bf16).astype(f32)
        rows += [high, middle, value - high - middle]
    target = positive[...]
    rows += [(target // 128).astype(f32), (target % 128).astype(f32), jnp.zeros((120, 128), f32)]
    stats = jnp.concatenate(rows).T.astype(bf16)
    need(0)
    top[:, :WIDTH], top[:, WIDTH:] = queries[0:HALF, :], stats[0:HALF]
    low[:, :WIDTH], low[:, WIDTH:] = queries[HALF:, :], stats[HALF:]
    ready(0, 1)


def call(kernel, outs, args, flops=0):
    outs = [jax.ShapeDtypeStruct(*o) for o in outs]
    size = sum(a.size * a.dtype.itemsize for a in [*args, *outs])
    n, m = len(args) - 1, len(outs)

    def body(scalar, *refs):
        operands, results, refs = refs[:n], refs[n : n + m], refs[n + m :]
        here, made, sem_in, sem_out = refs[:n], refs[n : n + m], refs[-2], refs[-1]
        fetched = [pltpu.make_async_copy(operands[i], here[i], sem_in.at[i]) for i in range(n)]
        for copy in fetched:
            copy.start()
        sent = [pltpu.make_async_copy(made[i], results[i], sem_out.at[i]) for i in range(m)]

        def need(*places):
            for i in places:
                fetched[i].wait()

        def ready(*places):
            for i in places:
                sent[i].start()

        kernel(scalar, *here, *made, need=need, ready=ready)
        for copy in sent:
            copy.wait()

    return pl.pallas_call(
        body,
        out_shape=outs,
        in_specs=[pl.BlockSpec(memory_space=s) for s in [SMEM] + [pl.ANY] * n],
        out_specs=[pl.BlockSpec(memory_space=pl.ANY)] * m,
        scratch_shapes=[
            *[VMEM(a.shape, a.dtype) for a in [*args[1:], *outs]],
            pltpu.SemaphoreType.DMA((n,)),
            pltpu.SemaphoreType.DMA((m,)),
        ],
        compiler_params=pltpu.CompilerParams(vmem_limit_bytes=60 * 1024 * 1024),
        cost_estimate=pl.CostEstimate(flops=flops, bytes_accessed=size, transcendentals=0),
    )(*args)


def on_device(queries, passages, row_lse, row_weight, positive):
    x, z, yl, yh, core = (lax.axis_index(a) for a in ("x", "z", "yl", "yh", "c"))
    rows, half = 2 * HALF, HALF
    flops = 2 * BLOCK * COLUMNS * WIDTH
    first_core = core == 0

    vectors = [value.reshape(1, rows) for value in (row_lse, row_weight, positive)]
    quarter = ((half, WIDTH), bf16)
    top, low, passage_own, passage_away = call(
        prepare,
        [((half, LOADED), bf16)] * 2 + [quarter] * 2,
        [yh.astype(jnp.int32).reshape(1), queries, passages, *vectors],
    )
    place = jnp.arange(COLUMNS, dtype=jnp.int32)
    owner = (yl * 4 + x) * 8 + (z + np.repeat(AROUND, half)) % 8
    column = (owner * rows + yh * half + place % half)[None, :]

    passage_back = flip(passage_away, "y", (2, 2))
    top_near, low_near = together(flip(top, "x", NEAR), flip(low, "y", NEAR))
    passage = jnp.concatenate([passage_own, passage_back])
    top, low = together(jnp.concatenate([top, top_near]), jnp.concatenate([low, low_near]))
    passage_near, top_far, low_far = together(exchange(passage, 0), flip(top, "x", FAR), flip(low, "y", FAR))
    ring, top, low = together(
        jnp.concatenate([passage, passage_near]),
        jnp.concatenate([top, top_far]),
        jnp.concatenate([low, low_far]),
    )
    got = exchange(ring, 1)
    top_near, low_near = together(flip(top, "y", NEAR), flip(low, "x", NEAR))
    top, low = together(jnp.concatenate([top, top_near]), jnp.concatenate([low, low_near]))
    top_far, low_far = flip(top, "y", FAR), flip(low, "x", FAR)
    ring = [passage, passage_near, got[:rows], got[rows:]]
    for turn in (0, 1):
        got = exchange(got, turn)
        ring += [got[:rows], got[rows:]]
    plus = (z + core) % 2 == 0

    def in_order(blocks):
        blocks = list(blocks)
        for i in (1, 3, 5):
            one, two = blocks[i : i + 2]
            blocks[i : i + 2] = jnp.where(plus, one, two), jnp.where(plus, two, one)
        return blocks

    ring = in_order(ring)
    p_same = jnp.concatenate([b[:half] for b in ring])
    p_other = jnp.concatenate([b[half:] for b in ring])

    def pick(own, near, far, opposite, axis):
        same = jnp.concatenate([own, jnp.where(first_core, near, far)], axis=axis)
        other = jnp.concatenate([opposite, jnp.where(first_core, far, near)], axis=axis)
        return same, other

    top_same, top_other = pick(top[:BLOCK], top[BLOCK:], top_far[:BLOCK], top_far[BLOCK:], 0)
    low_same, low_other = [], []
    for part in (low, low_far):
        part = part.reshape(2, 4, half, LOADED)
        same, other = pick(part[:, 0:1], part[:, 1:2], part[:, 2:3], part[:, 3:4], 1)
        low_same.append(same.reshape(BLOCK, LOADED))
        low_other.append(other.reshape(BLOCK, LOADED))
    q_same = [top_same, jnp.concatenate(low_same)]
    q_other = [top_other, jnp.concatenate(low_other)]
    stats = [q[:, WIDTH:].astype(f32) for q in q_same]
    q_same = [q[:, :WIDTH] for q in q_same]
    q_other = [q[:, :WIDTH] for q in q_other]

    def swapped(scores, shape, axis):
        scores = lax.ppermute(scores, "c", [(0, 1), (1, 0)]).reshape(shape)
        blocks = [lax.slice_in_dim(scores, i, i + 1, axis=axis) for i in (0, 2, 1, 3)]
        return jnp.concatenate(blocks, axis=axis).reshape(COLUMNS, COLUMNS)

    grads = []
    for same, other, stat, shape, axis in zip(
        q_same, q_other, stats, ((2, 4, half, COLUMNS), (4, rows, COLUMNS)), (1, 0)
    ):
        partial_value = dot(same, p_same, ((1,), (1,))) + dot(other, p_other, ((1,), (1,)))
        scores = partial_value + swapped(partial_value, shape, axis)
        lse = stat[:, 0:1] + stat[:, 1:2] + stat[:, 2:3]
        weight = stat[:, 3:4] + stat[:, 4:5] + stat[:, 5:6]
        target = (stat[:, 6:7] * 128 + stat[:, 7:8]).astype(jnp.int32)
        is_positive = (column == target).astype(f32)
        grads.append((weight * (jnp.exp(inv_temp * scores - lse) - is_positive)).astype(bf16))

    w_same = [dot(g, p_same, ((1,), (0,))) for g in grads]
    w_other = [dot(g, p_other, ((1,), (0,))) for g in grads]
    v_same = dot(grads[0], q_same[0], ((0,), (0,))) + dot(grads[1], q_same[1], ((0,), (0,)))
    v_other = dot(grads[0], q_other[0], ((0,), (0,))) + dot(grads[1], q_other[1], ((0,), (0,)))
    parts = [
        jnp.concatenate([v_same[i * half : (i + 1) * half], v_other[i * half : (i + 1) * half]]) for i in range(8)
    ]

    near, far = w_same[0][BLOCK:], w_other[0][BLOCK:]
    top_own, top_near = w_same[0][:BLOCK], jnp.where(first_core, near, far)
    top_send = jnp.concatenate([jnp.where(first_core, far, near), w_other[0][:BLOCK]]).astype(bf16)
    same, other = w_same[1].reshape(4, rows, WIDTH), w_other[1].reshape(4, rows, WIDTH)
    low_all = jnp.concatenate([same, other], axis=1)
    low_own, low_near, low_send = low_all[0], low_all[1], low_all[2:].reshape(2 * BLOCK, WIDTH).astype(bf16)
    top_got, low_got = flip(top_send, "y", FAR), flip(low_send, "x", FAR)
    parts = dict(zip(AROUND.tolist(), parts))
    up, down = together(shift(parts[4].astype(bf16), 1), shift(parts[5].astype(bf16), -1))
    up, down = together((parts[3] + up).astype(bf16), (parts[6] + down).astype(bf16))
    up, down, top_got, low_got = together(shift(up, 1), shift(down, -1), top_got, low_got)
    up, down = together((parts[2] + up).astype(bf16), (parts[7] + down).astype(bf16))
    up, down = together(shift(up, 1), shift(down, -1))
    top_send, low_send = together(
        (top_near + top_got[BLOCK:]).astype(bf16), (low_near + low_got[BLOCK:]).astype(bf16)
    )
    top_last, low_last = together(flip(top_send, "y", NEAR), flip(low_send, "x", NEAR))
    top = top_own + top_got[:BLOCK] + top_last
    low = low_own + low_got[:BLOCK] + low_last
    one, three = low[half:rows], low[rows + half :]
    low_near = jnp.where(first_core, one, three)
    low_send = jnp.concatenate([jnp.where(first_core, three, one), low[rows : rows + half]]).astype(bf16)
    up = shift((parts[1] + up).astype(bf16), 1)
    top_send, low_send = together(top[rows:].astype(bf16), low_send)
    top_got, low_got = together(flip(top_send, "x", FAR), flip(low_send, "y", FAR))
    passage_sum = (inv_temp * (parts[0] + up + down)).astype(bf16)
    passage_own = passage_sum[:half]
    passage_back = flip(passage_sum[half:], "y", (2, 2))
    top_last = flip((top[half:rows] + top_got[half:]).astype(bf16), "x", NEAR)
    low_last = flip((low_near + low_got[half:]).astype(bf16), "y", NEAR)
    top_last, low_last = together(top_last, low_last)
    passage_grad = jnp.where(
        yh == 0,
        jnp.concatenate([passage_own, passage_back]),
        jnp.concatenate([passage_back, passage_own]),
    )
    top = (inv_temp * (top[:half] + top_got[:half] + top_last)).astype(bf16)
    low = (inv_temp * (low[:half] + low_got[:half] + low_last)).astype(bf16)
    query_grad = jnp.concatenate([top, low])
    return query_grad, passage_grad


def solution(mesh):
    split = Mesh(mesh.devices.reshape(2, 4, 8, 2, 2), ("yl", "x", "z", "yh", "c"))
    matrix, vector = P(ROWS_SPEC, FEATURES_SPEC), P(ROWS_SPEC)
    return jax.shard_map(
        on_device,
        mesh=split,
        in_specs=(matrix, matrix, vector, vector, vector),
        out_specs=(matrix, matrix),
        check_vma=False,
    )
```
